32 devices in a mesh: group: 2 (over x), inst: 8 (over z, y), tp: 2 (over core).
Axes of the slice: x: 2, y: 2, z: 4, core: 2. Of those that a mesh axis runs over, the one named last changes fastest.
Arguments:
- kv_pool: bfloat16 [2560, 16, 2, 1024], P(('group', 'inst'), None, None, 'tp'), parts along dimension 0, may hold values from -5 to 5
- page_table: int32 [160, 16], P(('group', 'inst')), parts along dimension 0, may hold values from 0 to 159, as said below
- lengths: int32 [160], P(('group', 'inst')), parts along dimension 0, may hold values from 0 to 252, as said below
- move_source: int32 [16, 4, 2], P(('group', 'inst')), parts along dimension 0, may hold values from -1 to 9, as said below
- move_slot: int32 [16, 4, 2], P(('group', 'inst')), parts along dimension 0, may hold values from -1 to 9, as said below
- queries: bfloat16 [4, 160, 8192], P(None, ('group', 'inst'), 'tp'), parts along dimension 1, may hold values from -5 to 5
- new_kv: bfloat16 [4, 160, 2, 1024], P(None, ('group', 'inst'), None, 'tp'), parts along dimension 1, may hold values from -5 to 5
Outputs:
- attended: bfloat16 [4, 160, 8192], P(None, ('group', 'inst'), 'tp'), parts along dimension 1
- cache_after: bfloat16 [2560, 16, 2, 1024], P(('group', 'inst'), None, None, 'tp'), parts along dimension 0
The draws below stay inside these ranges and needn't reach their ends.
There are 2 independent parts, one for each index of `group`. The reference program is written for one: setup_inputs(seed, part) draws one part's arguments, and reference() takes and returns one part's arrays. A program takes and returns all parts, laid end to end along the dimension named above; each array names one. Nothing has to cross between parts.
Inputs may be any that keep to these rules, and one draw needn't show every extreme that they name: `page_table`: the 16 entries of the 10 rows of one instance name each of that instance's 160 pages once. `lengths`: every length plus 4 fits the row's 16 pages. At step s instance i sends at most one row to each side e, the live row in slot move_source[i, s, e] (-1: none), to instance i + 1 modulo 8 for side 0 and i - 1 modulo 8 for side 1. A slot sends at most once, a slot that a row leaves stays empty, and a row that arrives is never sent on. `move_slot`: the receiving slot is empty (length 0) until the row arrives and receives no other row (-1 where nothing is sent).
All inputs are finite; a program needn't handle non-finite values.
Results may differ from the reference program's by a relative error of at most 0.0039.
Values may be sent and summed in bfloat16 or wider, within the bound.
A program may use at most 128 MiB of HBM per device.

```python
import jax
import jax.numpy as jnp
from jax import lax

QH = 64
KVH = 8
HD = 128
PAGE = 16
CTX_PAGES = 16
SLOTS = 10
STEPS = 4
INSTS = 8
ROWS = 80
PAGES = 160
LMAX = 252
LIVE_LIGHT = 2


def permute_slots(sub_key):
    return jax.random.permutation(sub_key, SLOTS)


def permute_pages(sub_key):
    return jax.random.permutation(sub_key, PAGES)


def plan(key):
    base = jax.random.fold_in(key, 201)
    parity = jax.random.randint(jax.random.fold_in(base, 1), (), 0, 2)
    inst_ids = jnp.arange(INSTS, dtype=jnp.int32)
    is_busy = (inst_ids + parity) % 2 == 0
    slot_order = jax.vmap(permute_slots)(jax.random.split(jax.random.fold_in(base, 2), INSTS)).astype(jnp.int32)
    long_len = jax.random.randint(jax.random.fold_in(base, 3), (INSTS, SLOTS), LMAX // 2, LMAX + 1)
    long_len = long_len.at[:, 0].set(LMAX)
    short_len = jax.random.randint(jax.random.fold_in(base, 4), (INSTS, SLOTS), 1, LMAX // 4 + 1)
    logical = jnp.arange(SLOTS, dtype=jnp.int32)[None, :]
    light_len = jnp.where(logical < LIVE_LIGHT, short_len, 0)
    logical_len = jnp.where(is_busy[:, None], long_len, light_len).astype(jnp.int32)
    lengths = jnp.zeros((INSTS, SLOTS), jnp.int32).at[inst_ids[:, None], slot_order].set(logical_len)
    side_bit = jnp.arange(2, dtype=jnp.int32)[None, None, :]
    step_grid = jnp.arange(STEPS, dtype=jnp.int32)[None, :, None]
    dest = jnp.where(side_bit == 0, (inst_ids[:, None, None] + 1) % INSTS, (inst_ids[:, None, None] + INSTS - 1) % INSTS)
    dest = jnp.broadcast_to(dest, (INSTS, STEPS, 2))
    dest_logical = jnp.broadcast_to(LIVE_LIGHT + 2 * step_grid + side_bit, (INSTS, STEPS, 2))
    dest_slot = slot_order[dest, dest_logical]
    source = slot_order[:, :2 * STEPS].reshape(INSTS, STEPS, 2)
    busy = is_busy[:, None, None]
    move_source = jnp.where(busy, source, -1).astype(jnp.int32)
    move_slot = jnp.where(busy, dest_slot, -1).astype(jnp.int32)
    return (lengths.reshape(INSTS * SLOTS), move_source, move_slot)


def draw_lengths(key, part):
    return plan(key)[0]


def draw_move_source(key, part):
    return plan(key)[1]


def draw_move_slot(key, part):
    return plan(key)[2]


def draw_page_table(key, part):
    key = jax.random.fold_in(key, 3)
    tables = jax.vmap(permute_pages)(jax.random.split(key, INSTS))
    return tables.reshape(INSTS * SLOTS, CTX_PAGES).astype(jnp.int32)


def draw_kv_pool(key, part):
    key = jax.random.fold_in(key, 7)
    shape = (INSTS * PAGES, PAGE, 2, KVH * HD)
    values = jnp.clip(jax.random.normal(key, shape, jnp.float32), -5.0, 5.0)
    return values.astype(jnp.bfloat16)


def draw_queries(key, part):
    key = jax.random.fold_in(key, 9)
    shape = (STEPS, INSTS * SLOTS, QH * HD)
    values = jnp.clip(jax.random.normal(key, shape, jnp.float32), -5.0, 5.0)
    return values.astype(jnp.bfloat16)


def block_scale(own_key, shape, pieces, low, high):
    def one(position, parts):
        steps = jax.random.uniform(jax.random.fold_in(jax.random.fold_in(own_key, 6), position), (parts,), jnp.float32, low / len(pieces), high / len(pieces))
        return jnp.repeat(jnp.exp(steps), shape[position] // parts).reshape((-1,) + (1,) * (len(shape) - position - 1))

    gain = one(*pieces[0])
    for cut in pieces[1:]:
        gain = gain * one(*cut)
    return gain


def noise(stream_key, dims, deviation, bound, pieces=(), kind=jnp.bfloat16):
    values = deviation * jax.random.normal(stream_key, dims, jnp.float32)
    if pieces:
        values = values * block_scale(stream_key, dims, pieces, -0.22, 0.18)
    return jnp.clip(values, -bound, bound).astype(kind)


def setup_inputs(seed: int = 0, part: int = 0) -> dict:
    splits = jax.random.split(jax.random.key(seed), 8)
    part_splits = jax.random.split(jax.random.fold_in(splits[7], part), 8)
    return {
        "kv_pool": draw_kv_pool(jax.random.fold_in(jax.random.fold_in(splits[7], part), 71), part),
        "page_table": draw_page_table(jax.random.fold_in(jax.random.fold_in(splits[7], part), 71), part),
        "lengths": draw_lengths(jax.random.fold_in(jax.random.fold_in(splits[7], part), 71), part),
        "move_source": draw_move_source(jax.random.fold_in(jax.random.fold_in(splits[7], part), 71), part),
        "move_slot": draw_move_slot(jax.random.fold_in(jax.random.fold_in(splits[7], part), 71), part),
        "queries": draw_queries(jax.random.fold_in(jax.random.fold_in(splits[7], part), 71), part),
        "new_kv": noise(part_splits[6], (STEPS, ROWS, 2, KVH * HD), 1.0, 5.0, ((1, 8), (3, 2))),
    }


def reference(kv_pool, page_table, lengths, move_source, move_slot, queries, new_kv):
    group_size = QH // KVH
    context = CTX_PAGES * PAGE
    kv_width = KVH * HD
    row_count = INSTS * SLOTS
    row_ids = jnp.arange(row_count, dtype=jnp.int32)
    step_ids = jnp.arange(STEPS, dtype=jnp.int32)
    is_moving = move_source >= 0
    inst_ids = jnp.arange(INSTS, dtype=jnp.int32)[:, None, None]
    side_bits = jnp.arange(2, dtype=jnp.int32)[None, None, :]
    receiver = jnp.where(side_bits == 0, (inst_ids + 1) % INSTS, (inst_ids + INSTS - 1) % INSTS).astype(jnp.int32)
    receiver = jnp.broadcast_to(receiver, move_source.shape)
    anchor = inst_ids * SLOTS + move_source
    anchor = jnp.where(is_moving, anchor, row_count).astype(jnp.int32).reshape(-1)
    target = (receiver * SLOTS + move_slot).astype(jnp.int32).reshape(-1)
    step_grid = jnp.broadcast_to(step_ids[None, :, None], move_source.shape).reshape(-1)
    move_step = jnp.full((row_count,), STEPS, jnp.int32).at[anchor].set(step_grid, mode="drop")
    move_to = row_ids.at[anchor].set(target, mode="drop")
    places = jnp.where(step_ids[None, :] >= move_step[:, None], move_to[:, None], row_ids[:, None]).astype(jnp.int32)
    global_pages = (page_table + (row_ids // SLOTS)[:, None] * PAGES).astype(jnp.int32)

    def one_row(items):
        length, pages, row_places, moved_at = items
        initial = kv_pool[pages].reshape(context, 2, kv_width)
        fresh_kv = new_kv[step_ids, row_places]
        start = (length, jnp.int32(0), jnp.int32(0))
        full_cache = lax.dynamic_update_slice(initial, fresh_kv, start)
        existing = lax.dynamic_slice(initial, start, (STEPS, 2, kv_width))
        early_kv = jnp.where((step_ids < moved_at)[:, None, None], fresh_kv, existing)
        source_cache = lax.dynamic_update_slice(initial, early_kv, start)
        key_rows = full_cache[:, 0].reshape(context, KVH, HD).astype(jnp.float32)
        value_rows = full_cache[:, 1].reshape(context, KVH, HD).astype(jnp.float32)
        query_rows = queries[step_ids, row_places].reshape(STEPS, KVH, group_size, HD).astype(jnp.float32)
        scores = jnp.einsum("skgd,tkd->skgt", query_rows, key_rows) * (HD ** -0.5)
        visible = jnp.arange(context, dtype=jnp.int32)[None, :] <= (length + step_ids)[:, None]
        scores = jnp.where(visible[:, None, None, :], scores, -jnp.inf)
        row_max = jnp.max(scores, axis=-1, keepdims=True)
        exp_terms = jnp.exp(scores - row_max)
        row_total = jnp.sum(exp_terms, axis=-1)
        weights = lax.optimization_barrier(exp_terms.astype(jnp.bfloat16)).astype(jnp.float32)
        result = jnp.einsum("skgt,tkd->skgd", weights, value_rows) / row_total[..., None]
        result = jnp.where(length > 0, result, 0.0)
        result = result.reshape(STEPS, QH * HD).astype(jnp.bfloat16)
        return result, full_cache.reshape(CTX_PAGES, PAGE, 2, kv_width), source_cache.reshape(CTX_PAGES, PAGE, 2, kv_width)

    results, full_caches, source_caches = lax.map(one_row, (lengths, global_pages, places, move_step))
    attended = jnp.zeros((STEPS, row_count, QH * HD), jnp.bfloat16)
    attended = attended.at[jnp.broadcast_to(step_ids[None, :], places.shape), places].add(results)
    final_place = places[:, STEPS - 1]
    final_pages = page_table[final_place] + (final_place // SLOTS)[:, None] * PAGES
    is_live = lengths > 0
    final_pages = jnp.where(is_live[:, None], final_pages, INSTS * PAGES).astype(jnp.int32)
    cache_after = kv_pool.at[final_pages].set(full_caches, mode="drop")
    left_pages = jnp.where((is_live & (move_step < STEPS))[:, None], global_pages, INSTS * PAGES).astype(jnp.int32)
    cache_after = cache_after.at[left_pages].set(source_caches, mode="drop")
    return attended, cache_after
```

```python
import functools

import jax
import jax.numpy as jnp
from jax import lax
from jax.experimental import pallas as pl
from jax.experimental.pallas import tpu as pltpu
from jax.sharding import PartitionSpec as P

HD = 128
SMEM = pl.BlockSpec(memory_space=pltpu.SMEM)
VMEM = pl.BlockSpec(memory_space=pltpu.VMEM)
ANY = pl.BlockSpec(memory_space=pl.ANY)


def pack_kernel(step, table, lengths, source, pool, fresh, left, right, page_sem, token_sem):
    ctx_pages = table.shape[1]
    page_len = pool.shape[1]
    outs = (left, right)

    def one_page(p, carry):
        for side in range(2):
            slot = jnp.maximum(source[0, step, side], 0)
            pltpu.make_async_copy(
                pool.at[table[slot, p]],
                outs[side].at[pl.ds(p * page_len, page_len)],
                page_sem.at[side],
            ).start()
        return carry

    lax.fori_loop(0, ctx_pages, one_page, 0)
    for side in range(2):
        pltpu.make_async_copy(outs[side], outs[side], page_sem.at[side]).wait()
    copies = []
    for side in range(2):
        slot = jnp.maximum(source[0, step, side], 0)
        for early in range(step):
            copies.append(
                pltpu.make_async_copy(
                    fresh.at[early, slot],
                    outs[side].at[lengths[slot] + early],
                    token_sem.at[side, early],
                )
            )
    for copy in copies:
        copy.start()
    for copy in copies:
        copy.wait()


def pack(step, table, lengths, source, pool, fresh):
    tokens = table.shape[1] * pool.shape[1]
    row = jax.ShapeDtypeStruct((tokens,) + pool.shape[2:], pool.dtype)
    nbytes = 4 * tokens * pool.shape[2] * pool.shape[3] * 2
    return pl.pallas_call(
        functools.partial(pack_kernel, step),
        out_shape=(row, row),
        in_specs=[SMEM, SMEM, SMEM, ANY, ANY],
        out_specs=(ANY, ANY),
        scratch_shapes=[pltpu.SemaphoreType.DMA((2,)), pltpu.SemaphoreType.DMA((2, fresh.shape[0]))],
        cost_estimate=pl.CostEstimate(flops=0, bytes_accessed=nbytes, transcendentals=0),
    )(table, lengths, source, pool, fresh)


def attend(rows, query, out, slot, base, first, low, high):
    kv_heads, columns, _ = rows.shape
    total_rows = query.shape[2]
    steps = out.shape[0]
    group = total_rows // steps
    skip = first * group
    shape = (total_rows - skip, columns)
    row_step = lax.broadcasted_iota(jnp.int32, shape, 0) // group + first
    column = lax.broadcasted_iota(jnp.int32, shape, 1)
    seen = (column % 2 == 0) & (column // 2 <= base + row_step)
    step_of = lax.broadcasted_iota(jnp.int32, (shape[0], HD), 0) // group + first
    live = (step_of >= low) & (step_of < high)
    chosen = lax.broadcasted_iota(jnp.int32, (out.shape[1], HD), 0) == slot
    for head in range(kv_heads):
        matrix = rows[head]
        q = query[slot, head, skip:]
        scores = lax.dot_general(
            q, matrix, (((1,), (1,)), ((), ())), preferred_element_type=jnp.float32
        ) * HD ** (-0.5)
        scores = jnp.where(seen, scores, -jnp.inf)
        terms = jnp.exp(scores - jnp.max(scores, axis=1, keepdims=True))
        total = jnp.sum(terms, axis=1, keepdims=True)
        weights = pltpu.roll(terms, 1, 1).astype(jnp.bfloat16)
        result = jnp.dot(weights, matrix, preferred_element_type=jnp.float32) / total
        result = jnp.where(live, result, 0.0)
        for s in range(first, steps):
            for g in range(group):
                r = (s - first) * group + g
                lane = (head * group + g) * HD
                old = out[s, :, lane : lane + HD]
                out[s, :, lane : lane + HD] = jnp.where(chosen, result[r : r + 1], old)


def local_kernel(table, lengths, source, pool, fresh, query, cache, attended, rows, out, copy_sem, row_sem, token_sem):
    slots, ctx_pages = table.shape
    pages, page_len = pool.shape[:2]
    kv_heads = rows.shape[1]
    steps = fresh.shape[0]
    part = pages // slots

    def load_slot(c, carry):
        pltpu.make_async_copy(
            pool.at[pl.ds(c * part, part)], cache.at[pl.ds(c * part, part)], copy_sem
        ).start()

        def load_page(p, carry):
            for head in range(kv_heads):
                pltpu.make_async_copy(
                    pool.at[table[c, p], :, :, pl.ds(head * HD, HD)],
                    rows.at[c, head, pl.ds(p * page_len, page_len)],
                    row_sem.at[c],
                ).start()
            return carry

        return lax.fori_loop(0, ctx_pages, load_page, carry)

    lax.fori_loop(0, slots, load_slot, 0)

    def leave_step(c):
        leave = jnp.int32(steps)
        for s in range(steps):
            for side in range(2):
                leave = jnp.where(source[0, s, side] == c, s, leave)
        return jnp.where(lengths[c] > 0, leave, 0)

    def work(c, carry):
        pltpu.make_async_copy(rows.at[c], rows.at[c], row_sem.at[c]).wait()
        base = lengths[c]
        for s in range(steps):
            for head in range(kv_heads):
                rows[c, head, base + s] = fresh[s, c, :, head * HD : (head + 1) * HD]
        attend(
            rows.at[c].reshape(kv_heads, ctx_pages * page_len * 2, HD), query, out, c, base, 0, 0, leave_step(c)
        )
        return carry

    lax.fori_loop(0, slots, work, 0)
    pltpu.make_async_copy(cache, cache, copy_sem).wait()

    def token(c, s):
        pos = lengths[c] + s
        return pltpu.make_async_copy(
            fresh.at[s, c], cache.at[table[c, pos // page_len], pos % page_len], token_sem.at[c, s]
        )

    def start(c, carry):
        high = leave_step(c)
        for s in range(steps):

            @pl.when(s < high)
            def _():
                token(c, s).start()

        return carry

    def finish(c, carry):
        high = leave_step(c)
        for s in range(steps):

            @pl.when(s < high)
            def _():
                token(c, s).wait()

        return carry

    lax.fori_loop(0, slots, start, 0)
    attended[...] = out[...].astype(attended.dtype)
    lax.fori_loop(0, slots, finish, 0)


def local(table, lengths, source, pool, fresh, query):
    slots, ctx_pages = table.shape
    tokens = ctx_pages * pool.shape[1]
    kv_heads = query.shape[1]
    steps = fresh.shape[0]
    width = kv_heads * query.shape[2] // steps * HD
    return pl.pallas_call(
        local_kernel,
        out_shape=(
            jax.ShapeDtypeStruct(pool.shape, pool.dtype),
            jax.ShapeDtypeStruct((steps, slots, width), jnp.bfloat16),
        ),
        in_specs=[SMEM, SMEM, SMEM, ANY, VMEM, VMEM],
        out_specs=(ANY, VMEM),
        scratch_shapes=[
            pltpu.VMEM((slots, kv_heads, tokens, 2, HD), pool.dtype),
            pltpu.VMEM((steps, slots, width), jnp.float32),
            pltpu.SemaphoreType.DMA,
            pltpu.SemaphoreType.DMA((slots,)),
            pltpu.SemaphoreType.DMA((slots, steps)),
        ],
        compiler_params=pltpu.CompilerParams(vmem_limit_bytes=32 * 1024 * 1024),
        cost_estimate=pl.CostEstimate(flops=10**9, bytes_accessed=60 * 10**6, transcendentals=10**5),
    )(table, lengths, source, pool, fresh, query)


def arrive_kernel(step, table, meta_left, meta_right, left, right, fresh, query, cache_in, before, cache, attended, rows, out, page_sem, row_sem, token_sem):
    ctx_pages = table.shape[1]
    page_len = cache.shape[1]
    kv_heads = rows.shape[1]
    steps = fresh.shape[0]
    received = (left, right)
    metas = (meta_left, meta_right)

    def token(side, s, slot, base):
        pos = base + s
        return pltpu.make_async_copy(
            fresh.at[s, slot], cache.at[table[slot, pos // page_len], pos % page_len], token_sem.at[side, s]
        )

    for side in range(2):
        slot = metas[side][step, 0] - 1

        @pl.when(slot >= 0)
        def _():
            for head in range(kv_heads):
                pltpu.make_async_copy(
                    received[side].at[:, :, pl.ds(head * HD, HD)], rows.at[side, head], row_sem.at[side]
                ).start()

            def store_page(p, carry):
                pltpu.make_async_copy(
                    received[side].at[pl.ds(p * page_len, page_len)], cache.at[table[slot, p]], page_sem.at[side]
                ).start()
                return carry

            lax.fori_loop(0, ctx_pages, store_page, 0)

    out[...] = before[...].astype(jnp.float32)
    for side in range(2):
        slot = metas[side][step, 0] - 1
        base = metas[side][step, 1]

        @pl.when(slot >= 0)
        def _():
            pltpu.make_async_copy(rows.at[side], rows.at[side], row_sem.at[side]).wait()
            for s in range(step, steps):
                for head in range(kv_heads):
                    rows[side, head, base + s] = fresh[s, slot, :, head * HD : (head + 1) * HD]
            pltpu.make_async_copy(received[side], received[side], page_sem.at[side]).wait()
            for s in range(step, steps):
                token(side, s, slot, base).start()
            attend(
                rows.at[side].reshape(kv_heads, ctx_pages * page_len * 2, HD),
                query, out, slot, base, step, step, steps,
            )

    attended[...] = out[...].astype(attended.dtype)
    for side in range(2):
        slot = metas[side][step, 0] - 1
        base = metas[side][step, 1]

        @pl.when(slot >= 0)
        def _():
            for s in range(step, steps):
                token(side, s, slot, base).wait()


def arrive(step, table, meta_left, meta_right, left, right, fresh, query, cache, attended):
    tokens = left.shape[0]
    kv_heads = query.shape[1]
    steps = fresh.shape[0]
    return pl.pallas_call(
        functools.partial(arrive_kernel, step),
        out_shape=(
            jax.ShapeDtypeStruct(cache.shape, cache.dtype),
            jax.ShapeDtypeStruct(attended.shape, attended.dtype),
        ),
        in_specs=[SMEM, SMEM, SMEM, ANY, ANY, VMEM, VMEM, ANY, VMEM],
        out_specs=(ANY, VMEM),
        input_output_aliases={7: 0},
        scratch_shapes=[
            pltpu.VMEM((2, kv_heads, tokens, 2, HD), cache.dtype),
            pltpu.VMEM(attended.shape, jnp.float32),
            pltpu.SemaphoreType.DMA((2,)),
            pltpu.SemaphoreType.DMA((2,)),
            pltpu.SemaphoreType.DMA((2, steps)),
        ],
        compiler_params=pltpu.CompilerParams(vmem_limit_bytes=32 * 1024 * 1024),
        cost_estimate=pl.CostEstimate(flops=10**8, bytes_accessed=10 * 10**6, transcendentals=10**5),
    )(table, meta_left, meta_right, left, right, fresh, query, cache, attended)


def body(kv_pool, page_table, lengths, move_source, move_slot, queries, new_kv):
    slots = page_table.shape[0]
    steps = queries.shape[0]
    kv_heads = kv_pool.shape[3] // HD
    group = queries.shape[2] // HD // kv_heads
    count = lax.axis_size("inst")

    def shift(value, by):
        return lax.ppermute(value, "inst", [(i, (i + by) % count) for i in range(count)])

    arrived = []
    for step in range(steps):
        up, down = pack(step, page_table, lengths, move_source, kv_pool, new_kv)
        if step == 0:
            up, down, queries, move_slot = lax.optimization_barrier((up, down, queries, move_slot))
        arrived.append((shift(up, 1), shift(down, -1)))
    length = lengths[jnp.maximum(move_source[0], 0)]
    meta = jnp.stack([jnp.where(move_source[0] >= 0, move_slot[0] + 1, 0), length], axis=2)
    meta_left = shift(meta[:, 0], 1)
    meta_right = shift(meta[:, 1], -1)
    query = queries.reshape(steps, slots, kv_heads, group, HD).transpose(1, 2, 0, 3, 4)
    query = query.reshape(slots, kv_heads, steps * group, HD)
    cache, attended = local(page_table, lengths, move_source, kv_pool, new_kv, query)
    for step in range(steps):
        cache, attended = arrive(
            step, page_table, meta_left, meta_right, *arrived[step], new_kv, query, cache, attended
        )
    return attended, cache


def solution(mesh):
    in_specs = (
        P(("group", "inst"), None, None, "tp"),
        P(("group", "inst"), None),
        P(("group", "inst")),
        P(("group", "inst"), None, None),
        P(("group", "inst"), None, None),
        P(None, ("group", "inst"), "tp"),
        P(None, ("group", "inst"), None, "tp"),
    )
    out_specs = (P(None, ("group", "inst"), "tp"), P(("group", "inst"), None, None, "tp"))
    return jax.shard_map(body, mesh=mesh, in_specs=in_specs, out_specs=out_specs, check_vma=False)
```

```python
import functools

import jax
import jax.numpy as jnp
from jax import lax
from jax.experimental import pallas as pl
from jax.experimental.pallas import tpu as pltpu
from jax.sharding import PartitionSpec as P

HD = 128
SMEM = pl.BlockSpec(memory_space=pltpu.SMEM)
VMEM = pl.BlockSpec(memory_space=pltpu.VMEM)
ANY = pl.BlockSpec(memory_space=pl.ANY)


def pack_kernel(chunk, table, lengths, source, target, pool, fresh, left, right, page_sem):
    ctx_pages = table.shape[1]
    page_len = pool.shape[1]
    tokens = ctx_pages * page_len
    outs = (left, right)

    def one_page(p, carry):
        for side in range(2):
            for k, step in enumerate(chunk):
                slot = jnp.maximum(source[0, step, side], 0)
                pltpu.make_async_copy(
                    pool.at[table[slot, p]],
                    outs[side].at[pl.ds(k * tokens + p * page_len, page_len)],
                    page_sem.at[side],
                ).start()
        return carry

    lax.fori_loop(0, ctx_pages, one_page, 0)
    for side in range(2):
        filled = outs[side].at[pl.ds(0, len(chunk) * tokens)]
        pltpu.make_async_copy(filled, filled, page_sem.at[side]).wait()
        for k, step in enumerate(chunk):
            slot = jnp.maximum(source[0, step, side], 0)
            for early in range(step):
                outs[side][k * tokens + lengths[slot] + early] = fresh[early, slot]
        if 0 in chunk:
            lane = lax.broadcasted_iota(jnp.int32, pool.shape[2:], 1)
            meta = jnp.zeros(pool.shape[2:], jnp.int32)
            for s in range(source.shape[1]):
                moved = source[0, s, side]
                place = jnp.where(moved >= 0, target[0, s, side] + 1, 0)
                meta = jnp.where(lane == 2 * s, place, meta)
                meta = jnp.where(lane == 2 * s + 1, lengths[jnp.maximum(moved, 0)], meta)
            outs[side][len(chunk) * tokens] = meta.astype(jnp.float32).astype(pool.dtype)


def pack(chunk, table, lengths, source, target, pool, fresh):
    tokens = len(chunk) * table.shape[1] * pool.shape[1]
    row = jax.ShapeDtypeStruct((tokens + (0 in chunk),) + pool.shape[2:], pool.dtype)
    nbytes = 4 * tokens * pool.shape[2] * pool.shape[3] * 2
    return pl.pallas_call(
        functools.partial(pack_kernel, chunk),
        out_shape=(row, row),
        in_specs=[SMEM, SMEM, SMEM, SMEM, ANY, ANY if chunk == (0,) else VMEM],
        out_specs=(VMEM, VMEM),
        scratch_shapes=[pltpu.SemaphoreType.DMA((2,))],
        compiler_params=pltpu.CompilerParams(vmem_limit_bytes=32 * 1024 * 1024),
        cost_estimate=pl.CostEstimate(flops=0, bytes_accessed=nbytes, transcendentals=0),
    )(table, lengths, source, target, pool, fresh)


def attend(rows, query, out, slot, base, first, low, high):
    kv_heads, columns, _ = rows.shape
    total_rows = query.shape[2]
    steps = out.shape[1]
    group = total_rows // steps
    skip = first * group
    shape = (total_rows - skip, columns)
    row_step = lax.broadcasted_iota(jnp.int32, shape, 0) // group + first
    column = lax.broadcasted_iota(jnp.int32, shape, 1)
    seen = (column % 2 == 0) & (column // 2 <= base + row_step)
    step_of = lax.broadcasted_iota(jnp.int32, (shape[0], HD), 0) // group + first
    live = (step_of >= low) & (step_of < high)
    results = []
    scores = [
        lax.dot_general(
            query[slot, head, skip:], rows[head], (((1,), (1,)), ((), ())), preferred_element_type=jnp.float32
        )
        for head in range(kv_heads)
    ]
    for head in range(kv_heads):
        score = jnp.where(seen, scores[head] * HD ** (-0.5), -jnp.inf)
        terms = jnp.exp(score - jnp.max(score, axis=1, keepdims=True))
        total = jnp.sum(terms, axis=1, keepdims=True)
        weights = pltpu.roll(terms, 1, 1).astype(jnp.bfloat16)
        result = jnp.dot(weights, rows[head], preferred_element_type=jnp.float32) / total
        results.append(jnp.where(live, result, 0.0))
    for head in range(kv_heads):
        for s in range(first, steps):
            for g in range(group):
                r = (s - first) * group + g
                lane = (head * group + g) * HD
                out[slot, s : s + 1, lane : lane + HD] = results[head][r : r + 1]


def local_kernel(table, lengths, source, pool, fresh, query, cache, attended, rows, held, out, out_sem, held_sem, row_sem):
    slots, ctx_pages = table.shape
    page_len = pool.shape[1]
    kv_heads = rows.shape[1]
    steps = fresh.shape[0]

    def load_slot(c, carry):
        def load_page(p, carry):
            pltpu.make_async_copy(
                pool.at[table[c, p]], held.at[c, pl.ds(p * page_len, page_len)], held_sem.at[c]
            ).start()
            return carry

        return lax.fori_loop(0, ctx_pages, load_page, carry)

    lax.fori_loop(0, slots, load_slot, 0)

    def leave_step(c):
        leave = jnp.int32(steps)
        for s in range(steps):
            for side in range(2):
                leave = jnp.where(source[0, s, side] == c, s, leave)
        return jnp.where(lengths[c] > 0, leave, 0)

    def split(c):
        pltpu.make_async_copy(held.at[c], held.at[c], held_sem.at[c]).wait()
        high = leave_step(c)
        for s in range(steps):

            @pl.when(s < high)
            def _():
                held[c, lengths[c] + s] = fresh[s, c]

        for head in range(kv_heads):
            pltpu.make_async_copy(
                held.at[c, :, :, pl.ds(head * HD, HD)], rows.at[c % 2, head], row_sem.at[c % 2]
            ).start()

        def store_page(p, carry):
            pltpu.make_async_copy(
                held.at[c, pl.ds(p * page_len, page_len)], cache.at[table[c, p]], out_sem
            ).start()
            return carry

        lax.fori_loop(0, ctx_pages, store_page, 0)

    split(0)

    def work(c, carry):
        @pl.when(c + 1 < slots)
        def _():
            split(c + 1)

        buffer = rows.at[c % 2]
        pltpu.make_async_copy(buffer, buffer, row_sem.at[c % 2]).wait()
        attend(
            buffer.reshape(kv_heads, ctx_pages * page_len * 2, HD), query, out, c, lengths[c], 0, 0, leave_step(c)
        )
        attended[c] = out[c].astype(attended.dtype)
        return carry

    lax.fori_loop(0, slots, work, 0)
    pltpu.make_async_copy(cache, cache, out_sem).wait()


def local(table, lengths, source, pool, fresh, query):
    slots, ctx_pages = table.shape
    tokens = ctx_pages * pool.shape[1]
    kv_heads = query.shape[1]
    steps = fresh.shape[0]
    width = kv_heads * query.shape[2] // steps * HD
    return pl.pallas_call(
        local_kernel,
        out_shape=(
            jax.ShapeDtypeStruct(pool.shape, pool.dtype),
            jax.ShapeDtypeStruct((slots, steps, width), jnp.bfloat16),
        ),
        in_specs=[SMEM, SMEM, SMEM, ANY, VMEM, VMEM],
        out_specs=(ANY, VMEM),
        scratch_shapes=[
            pltpu.VMEM((2, kv_heads, tokens, 2, HD), pool.dtype),
            pltpu.VMEM((slots, tokens) + pool.shape[2:], pool.dtype),
            pltpu.VMEM((slots, steps, width), jnp.float32),
            pltpu.SemaphoreType.DMA,
            pltpu.SemaphoreType.DMA((slots,)),
            pltpu.SemaphoreType.DMA((2,)),
        ],
        compiler_params=pltpu.CompilerParams(vmem_limit_bytes=32 * 1024 * 1024),
        cost_estimate=pl.CostEstimate(flops=10**9, bytes_accessed=60 * 10**6, transcendentals=10**5),
    )(table, lengths, source, pool, fresh, query)


def arrive_kernel(chunk, table, meta_left, meta_right, left, right, fresh, query, cache_in, before, cache, attended, rows, held, out, out_sem, held_sem, row_sem):
    ctx_pages = table.shape[1]
    page_len = cache.shape[1]
    kv_heads = rows.shape[1]
    steps = fresh.shape[0]
    tokens = held.shape[1]
    items = []
    for k, step in enumerate(chunk):
        for received, meta in ((left, meta_left), (right, meta_right)):
            items.append(
                (len(items), step, received.at[pl.ds(k * tokens, tokens)], meta[step, 0] - 1, meta[step, 1])
            )

    for i, step, row, slot, base in items:

        @pl.when(slot >= 0)
        def _():
            pltpu.make_async_copy(row, held.at[i], held_sem.at[i]).start()
            for head in range(kv_heads):
                pltpu.make_async_copy(
                    row.at[:, :, pl.ds(head * HD, HD)], rows.at[i, head], row_sem.at[i]
                ).start()

    attended[...] = before[...]
    for i, step, row, slot, base in items:

        @pl.when(slot >= 0)
        def _():
            pltpu.make_async_copy(row, held.at[i], held_sem.at[i]).wait()
            for s in range(step, steps):
                held[i, base + s] = fresh[s, slot]

            def store_page(p, carry):
                pltpu.make_async_copy(
                    held.at[i, pl.ds(p * page_len, page_len)], cache.at[table[slot, p]], out_sem.at[i]
                ).start()
                return carry

            lax.fori_loop(0, ctx_pages, store_page, 0)
            pltpu.make_async_copy(rows.at[i], rows.at[i], row_sem.at[i]).wait()
            for s in range(step, steps):
                for head in range(kv_heads):
                    rows[i, head, base + s] = fresh[s, slot, :, head * HD : (head + 1) * HD]
            out[i] = jnp.zeros_like(out[i])
            attend(
                rows.at[i].reshape(kv_heads, tokens * 2, HD),
                query.at[pl.ds(slot, 1)], out.at[pl.ds(i, 1)], 0, base, step, step, steps,
            )
            attended[slot] = out[i].astype(attended.dtype)

    for i, step, row, slot, base in items:

        @pl.when(slot >= 0)
        def _():
            pltpu.make_async_copy(held.at[i], held.at[i], out_sem.at[i]).wait()


def arrive(chunk, table, meta_left, meta_right, left, right, fresh, query, cache, attended):
    kv_heads = query.shape[1]
    tokens = table.shape[1] * cache.shape[1]
    count = 2 * len(chunk)
    return pl.pallas_call(
        functools.partial(arrive_kernel, chunk),
        out_shape=(
            jax.ShapeDtypeStruct(cache.shape, cache.dtype),
            jax.ShapeDtypeStruct(attended.shape, attended.dtype),
        ),
        in_specs=[SMEM, SMEM, SMEM, ANY, ANY, VMEM, VMEM, ANY, VMEM],
        out_specs=(ANY, VMEM),
        input_output_aliases={7: 0},
        scratch_shapes=[
            pltpu.VMEM((count, kv_heads, tokens, 2, HD), cache.dtype),
            pltpu.VMEM((count, tokens) + cache.shape[2:], cache.dtype),
            pltpu.VMEM((count,) + attended.shape[1:], jnp.float32),
            pltpu.SemaphoreType.DMA((count,)),
            pltpu.SemaphoreType.DMA((count,)),
            pltpu.SemaphoreType.DMA((count,)),
        ],
        compiler_params=pltpu.CompilerParams(vmem_limit_bytes=32 * 1024 * 1024),
        cost_estimate=pl.CostEstimate(flops=10**8, bytes_accessed=10 * 10**6, transcendentals=10**5),
    )(table, meta_left, meta_right, left, right, fresh, query, cache, attended)


def body(kv_pool, page_table, lengths, move_source, move_slot, queries, new_kv):
    slots = page_table.shape[0]
    steps = queries.shape[0]
    kv_heads = kv_pool.shape[3] // HD
    group = queries.shape[2] // HD // kv_heads
    count = lax.axis_size("inst")

    def shift(value, by):
        return lax.ppermute(value, "inst", [(i, (i + by) % count) for i in range(count)])

    chunks = [(0,), tuple(range(1, steps - 1)), (steps - 1,)]
    arrived = []
    for chunk in chunks:
        up, down = pack(chunk, page_table, lengths, move_source, move_slot, kv_pool, new_kv)
        if chunk == chunks[0]:
            up, down, queries = lax.optimization_barrier((up, down, queries))
        if chunk == chunks[1]:
            query = queries.reshape(steps, slots, kv_heads, group, HD).transpose(1, 2, 0, 3, 4)
            query = query.reshape(slots, kv_heads, steps * group, HD)
            cache, attended = local(page_table, lengths, move_source, kv_pool, new_kv, query)
            lengths, attended = lax.optimization_barrier((lengths, attended))
        arrived.append((shift(up, 1), shift(down, -1)))
    meta_left, meta_right = (
        row[-1, 0, : 2 * steps].astype(jnp.int32).reshape(steps, 2) for row in arrived[0]
    )
    for chunk, received in zip(chunks, arrived):
        cache, attended = arrive(
            chunk, page_table, meta_left, meta_right, *received, new_kv, query, cache, attended
        )
    return attended.transpose(1, 0, 2), cache


def solution(mesh):
    in_specs = (
        P(("group", "inst"), None, None, "tp"),
        P(("group", "inst"), None),
        P(("group", "inst")),
        P(("group", "inst"), None, None),
        P(("group", "inst"), None, None),
        P(None, ("group", "inst"), "tp"),
        P(None, ("group", "inst"), None, "tp"),
    )
    out_specs = (P(None, ("group", "inst"), "tp"), P(("group", "inst"), None, None, "tp"))
    return jax.shard_map(body, mesh=mesh, in_specs=in_specs, out_specs=out_specs, check_vma=False)
```
